256 devices in a mesh: ctx: 16 (over x, y_hi, core), head: 16 (over z, y_lo).
Axes of the slice: x: 4, y: 4 (y_hi: 2, y_lo: 2; y = y_hi * 2 + y_lo), z: 8, core: 2. Of those that a mesh axis runs over, the one named last changes fastest.
Arguments:
- queries: bfloat16 [2048, 128, 128], P('ctx', 'head'), may hold values from -6 to 6
- query_rope: bfloat16 [2048, 128, 64], P('ctx', 'head'), may hold values from -100 to 100
- latent_cache: bfloat16 [2048, 576], P('ctx'), may hold values from -8 to 8
- key_up: bfloat16 [512, 16384], P(None, 'head'), may hold values from -0.25 to 0.25
- value_up: bfloat16 [512, 16384], P(None, 'head'), may hold values from -0.25 to 0.25
- out_proj: bfloat16 [16384, 7168], P('head', 'ctx'), may hold values from -0.75 to 0.75
Outputs:
- mixed_out: bfloat16 [2048, 7168], P(('ctx', 'head'))
The draws below stay inside these ranges and needn't reach their ends.
All inputs are finite; a program needn't handle non-finite values.
Results may differ from the reference program's by a relative error of at most 0.024.
Values may be sent and summed in bfloat16 or wider, within the bound.
A program may use at most 64 MiB of HBM per device.

```python
import jax
import jax.numpy as jnp
from jax import lax

D = 7168
H = 128
LAT = 512
ROPE = 64
NOPE = 128
VD = 128
HEAD_DEV = 8
TOKENS = 2048
N_HEAD = 16


def draw_latent_cache(key, part):
    key = jax.random.fold_in(key, 7)
    latent = jnp.clip(jax.random.normal(key, (TOKENS, LAT), jnp.float32), -6.0, 6.0)
    rope_part = jnp.clip(jax.random.normal(jax.random.fold_in(key, 1), (TOKENS, ROPE), jnp.float32), -6.0, 6.0)
    return jnp.concatenate([latent, rope_part], axis=1).astype(jnp.bfloat16)


def draw_query_rope(key, part):
    key = jax.random.fold_in(key, 13)
    result = jnp.clip(jax.random.normal(key, (TOKENS, H, ROPE), jnp.float32), -6.0, 6.0)
    return result.astype(jnp.bfloat16)


def shard_levels(stream_key, dims, pieces, low, top_value):
    gain = 1.0
    for position, parts in pieces:
        draws = jax.random.uniform(jax.random.fold_in(jax.random.fold_in(stream_key, 6), position), (parts,), jnp.float32, low / len(pieces), top_value / len(pieces))
        gain = gain * jnp.repeat(jnp.exp(draws), dims[position] // parts).reshape((-1,) + (1,) * (len(dims) - 1 - position))
    return gain


def normal_values(key, extent, scale, limit, cuts=(), kind=jnp.bfloat16):
    values = jax.random.normal(key, extent, jnp.float32) * scale
    if len(cuts) > 0:
        values = shard_levels(key, extent, cuts, -0.22, 0.18) * values
    return jnp.clip(values, min=-limit, max=limit).astype(kind)


def setup_inputs(seed: int = 0) -> dict:
    streams_of = jax.random.split(jax.random.key(seed), 7)
    queries = normal_values(streams_of[0], (TOKENS, H, NOPE), 1.0, 6.0, ((0, 16), (1, 16)))
    query_rope = draw_query_rope(jax.random.fold_in(streams_of[6], 71), 0)
    latent_cache = draw_latent_cache(jax.random.fold_in(streams_of[6], 71), 0)
    key_up = normal_values(streams_of[3], (LAT, H * NOPE), LAT ** -0.5, 0.25, ((1, 16),))
    value_up = normal_values(streams_of[4], (LAT, H * VD), LAT ** -0.5, 0.25, ((1, 16),))
    out_proj = normal_values(streams_of[5], (H * VD, D), 64 ** -0.5, 0.75, ((0, 16), (1, 16)))
    return dict(queries=queries, query_rope=query_rope, latent_cache=latent_cache, key_up=key_up, value_up=value_up, out_proj=out_proj)


MASKED = -1e30


def reference(queries, query_rope, latent_cache, key_up, value_up, out_proj):
    positions = jnp.arange(TOKENS, dtype=jnp.int32)
    allowed = positions[None, :] <= positions[:, None]
    latent = latent_cache[:, :LAT]
    rope_keys = latent_cache[:, LAT:]
    factor = (NOPE + ROPE) ** -0.5

    def one_head(head_index):
        key_cols = lax.dynamic_slice_in_dim(key_up, head_index * NOPE, NOPE, 1)
        value_cols = lax.dynamic_slice_in_dim(value_up, head_index * VD, VD, 1)
        key_rows = jnp.dot(latent, key_cols, preferred_element_type=jnp.float32).astype(jnp.bfloat16)
        value_rows = jnp.dot(latent, value_cols, preferred_element_type=jnp.float32).astype(jnp.bfloat16)
        query_nope = lax.dynamic_index_in_dim(queries, head_index, 1, keepdims=False)
        query_pos = lax.dynamic_index_in_dim(query_rope, head_index, 1, keepdims=False)
        scores = jnp.dot(query_nope, key_rows.T, preferred_element_type=jnp.float32)
        scores = (scores + jnp.dot(query_pos, rope_keys.T, preferred_element_type=jnp.float32)) * factor
        scores = jnp.where(allowed, scores, MASKED)
        row_max = jnp.max(scores, axis=1, keepdims=True)
        exps = jnp.exp(scores - row_max)
        weight_sum = jnp.sum(exps, axis=1, keepdims=True)
        head_out = jnp.dot(exps.astype(jnp.bfloat16), value_rows, preferred_element_type=jnp.float32) / weight_sum
        return head_out.astype(jnp.bfloat16)

    per_head = lax.map(one_head, jnp.arange(H, dtype=jnp.int32))
    attention = jnp.transpose(per_head, (1, 0, 2)).reshape(TOKENS, H * VD)
    group_width = HEAD_DEV * VD

    def add_group(total, group_index):
        cols = lax.dynamic_slice_in_dim(attention, group_index * group_width, group_width, 1)
        rows = lax.dynamic_slice_in_dim(out_proj, group_index * group_width, group_width, 0)
        partial_sum = jnp.dot(cols, rows, preferred_element_type=jnp.float32).astype(jnp.bfloat16)
        partial_sum = lax.optimization_barrier(partial_sum)
        return total + partial_sum.astype(jnp.float32), None

    total, _ = lax.scan(add_group, jnp.zeros((TOKENS, D), jnp.float32), jnp.arange(N_HEAD, dtype=jnp.int32))
    return total.astype(jnp.bfloat16)
```

```python
import functools

import jax
import jax.numpy as jnp
from jax import lax
from jax.experimental import pallas as pl
from jax.experimental.pallas import tpu as pltpu
from jax.sharding import PartitionSpec as P

LAT = 512
ROPE = 64
NOPE = 128
VD = 128
HEADS = 8
BLOCK = 128
COLS = 448
MASKED = -1e30
LOG2E = 1.4426950408889634
MESH = pl.DeviceIdType.MESH
BF16 = jnp.bfloat16
F32 = jnp.float32


def dot(a, b, contract):
    return lax.dot_general(a, b, ((contract[0], contract[1]), ((), ())), preferred_element_type=F32)


def kernel(
    q_hbm, qrt_hbm, latt_hbm, ku_hbm, vu_hbm, wt_hbm, out_ref,
    q_v, qrt_v, ku_v, vu_v, wt, qf, qa, qr, lt, kvr, kvt, m_s, l_s, acc, att,
    part, direct, sbuf, rbuf, dbuf, fin, landed,
    loc_sem, w_sem, p1_send, p1_recv, p3_send, p3_recv, swap_send, swap_recv,
    rs_send, rs_recv, d_send, d_recv, a_send, a_recv,
):
    c = lax.axis_index("ctx")
    h = lax.axis_index("head")
    x, yh, k = c // 4, (c // 2) % 2, c % 2
    z, yl = h // 2, h % 2

    def place(dx, flip=False):
        return ((x + dx) % 4) * 2 + ((1 - yh) if flip else yh)

    here = place(0)
    local = [
        pltpu.make_async_copy(src, dst, loc_sem.at[i])
        for i, (src, dst) in enumerate(
            [(latt_hbm, lt.at[here, k]), (q_hbm, q_v), (ku_hbm, ku_v), (qrt_hbm, qrt_v), (vu_hbm, vu_v), (wt_hbm, wt.at[yl])]
        )
    ]
    for copy in local:
        copy.start()

    core = (here * 2 + 1 - k, h)
    xp = (place(1) * 2 + k, h)
    xm = (place(3) * 2 + k, h)
    y_far = (place(0, True) * 2 + k, h)
    y_near = (place(0, True) * 2 + k, z * 2 + 1 - yl)
    y_low = (c, z * 2 + 1 - yl)
    y_cross = (here * 2 + 1 - k, z * 2 + 1 - yl)
    zp = (c, ((z + 1) % 8) * 2 + yl)
    zm = (c, ((z + 7) % 8) * 2 + yl)

    barrier = pltpu.get_barrier_semaphore()
    greeted = [((c + i) % 16, h) for i in range(1, 16)]
    greeted += [((c + i) % 16, z * 2 + 1 - yl) for i in range(16)]
    greeted += [(c, ((z + i) % 8) * 2 + yl) for i in range(1, 8)]
    for peer in greeted:
        pl.semaphore_signal(barrier, inc=1, device_id=peer, device_id_type=MESH)

    local[1].wait()
    local[2].wait()
    qf[...] = q_v[...].astype(F32).reshape(BLOCK * HEADS, NOPE)
    for i in range(HEADS):
        q_head = qf[pl.ds(i, BLOCK, stride=HEADS), :].astype(BF16)
        absorbed = dot(q_head, ku_v[:, i * NOPE : (i + 1) * NOPE], ((1,), (1,)))
        qa[i * BLOCK : (i + 1) * BLOCK] = absorbed.astype(BF16)
    local[3].wait()
    for i in range(HEADS):
        qr[i // 2, :, (i % 2) * BLOCK : (i % 2 + 1) * BLOCK] = qrt_v[i]
    local[0].wait()
    local[5].wait()

    pl.semaphore_wait(barrier, len(greeted))

    def gather(at, size, send, recv, y_peer):
        LO, HI, ALL = (0, size // 2), (size // 2, size // 2), (0, size)
        table = [
            (place(0), LO, y_peer, place(0, True)),
            (place(0), HI, y_peer, place(0, True)),
            (place(0), LO, xp, place(3)),
            (place(0), HI, xp, place(3)),
            (place(0), HI, xm, place(1)),
            (place(0), LO, xm, place(1)),
            (place(0, True), LO, xp, place(3, True)),
            (place(0, True), HI, xp, place(3, True)),
            (place(0, True), HI, xm, place(1, True)),
            (place(0, True), LO, xm, place(1, True)),
            (place(3), LO, xp, place(2)),
            (place(1), HI, xm, place(2)),
            (place(3, True), LO, xp, place(2, True)),
            (place(1, True), HI, xm, place(2, True)),
        ]
        table += [(spot, ALL, core, spot) for spot in (place(0), place(0, True), place(3), place(1), place(3, True), place(1, True), place(2), place(2, True))]

        def copy(e, index):
            _, rows, peer, _ = table[e]
            slot = (1 - k) if e >= 14 and index == 3 else k
            ref = at(table[e][index], slot, rows)
            return pltpu.make_async_remote_copy(
                src_ref=ref, dst_ref=ref, send_sem=send.at[e], recv_sem=recv.at[e],
                device_id=peer, device_id_type=MESH,
            )

        def start(*events):
            for e in events:
                copy(e, 0).start()

        def arrive(*events):
            for e in events:
                copy(e, 3).wait_recv()

        def drain():
            for e in range(len(table)):
                copy(e, 0).wait_send()

        return start, arrive, drain

    start1, arrive1, drain1 = gather(
        lambda i, s, rows: lt.at[i, s, pl.ds(rows[0], rows[1])], LAT + ROPE, p1_send, p1_recv, y_near
    )
    start3, arrive3, drain3 = gather(
        lambda i, s, rows: att.at[i, s, pl.ds(rows[0], rows[1])], BLOCK, p3_send, p3_recv, y_far
    )

    start1(2, 4, 0, 3, 5, 1, 14)
    w_copy = pltpu.make_async_remote_copy(
        src_ref=wt.at[yl], dst_ref=wt.at[yl], send_sem=w_sem.at[0], recv_sem=w_sem.at[1],
        device_id=y_low, device_id_type=MESH,
    )
    w_copy.start()

    def attend(group, diagonal):
        for b in range(4):
            tile = lt[group * 2 + b // 2, b % 2]
            kvt[:, b * BLOCK : (b + 1) * BLOCK] = tile[:LAT]
            kvr[b * BLOCK : (b + 1) * BLOCK] = tile.T

        def heads(i, _):
            rows = pl.ds(pl.multiple_of(i * 256, 256), 256)
            scores = dot(kvr[:, :LAT], qa[rows], ((1,), (1,)))
            scores += dot(kvr[:, LAT:], qr[i], ((1,), (0,)))
            scores = scores * ((NOPE + ROPE) ** -0.5 * LOG2E)
            if diagonal:
                key_pos = group * 512 + lax.broadcasted_iota(jnp.int32, (512, 256), 0)
                query_pos = c * BLOCK + lax.broadcasted_iota(jnp.int32, (512, 256), 1) % BLOCK
                scores = jnp.where(key_pos <= query_pos, scores, MASKED)
                new_max = jnp.max(scores, axis=0, keepdims=True)
                exps = jnp.exp2(scores - new_max)
                l_s[i] = jnp.sum(exps, axis=0, keepdims=True)
                acc[i] = dot(kvt[...], exps.astype(BF16), ((1,), (0,)))
            else:
                new_max = jnp.maximum(m_s[i], jnp.max(scores, axis=0, keepdims=True))
                rescale = jnp.exp2(m_s[i] - new_max)
                exps = jnp.exp2(scores - new_max)
                l_s[i] = l_s[i] * rescale + jnp.sum(exps, axis=0, keepdims=True)
                acc[i] = acc[i] * rescale + dot(kvt[...], exps.astype(BF16), ((1,), (0,)))
            m_s[i] = new_max
            return 0

        lax.fori_loop(0, 4, heads, 0)

    arrive1(2)
    start1(10)
    arrive1(4)
    start1(11)
    arrive1(0)
    start1(6, 9)
    arrive1(1)
    start1(8, 7, 15)
    arrive1(3, 5)
    start1(16, 17)
    arrive1(14, 15)
    attend(x, True)
    arrive1(6)
    start1(12)
    arrive1(8)
    start1(13)
    arrive1(7, 9)
    start1(18, 19)
    arrive1(10, 11)
    start1(20)
    arrive1(16, 18)

    @pl.when(x >= 1)
    def _():
        attend(x - 1, False)

    arrive1(12, 13)
    start1(21)
    arrive1(17, 19)

    @pl.when(x == 3)
    def _():
        attend(0, False)

    arrive1(20, 21)

    @pl.when(x >= 2)
    def _():
        attend(x - 2, False)

    local[4].wait()
    mine = jnp.where(k == yl, here, 8)
    for i in range(HEADS // 2):
        normed = (acc[i] / l_s[i]).T.astype(BF16)
        for j in range(2):
            cols = slice((2 * i + j) * VD, (2 * i + j + 1) * VD)
            att[mine, k, :, cols] = dot(
                normed[j * BLOCK : (j + 1) * BLOCK], vu_v[:, cols], ((1,), (0,))
            ).astype(BF16)

    def swap(half, outgoing):
        rows = pl.ds(half * 64, 64)
        return pltpu.make_async_remote_copy(
            src_ref=att.at[8, k, rows], dst_ref=att.at[here, (1 - k) if outgoing else k, rows],
            send_sem=swap_send.at[half], recv_sem=swap_recv.at[half], device_id=y_cross, device_id_type=MESH,
        )

    @pl.when(k == yl)
    def _():
        start3(2, 4, 0, 3, 5, 1, 14)

    @pl.when(k != yl)
    def _():
        swap(0, True).start()
        swap(1, True).start()
        swap(0, False).wait_recv()
        start3(2, 0)
        swap(1, False).wait_recv()
        start3(4, 1, 3, 5, 14)

    def spots(r):
        return ((place(0), place(0, True)), (place(3), place(1)), (place(3, True), place(1, True)), (place(2), place(2, True)))[r]

    def project(r, slot):
        spot = spots(r)[slot]
        product = dot(att[spot, 0], wt[0], ((1,), (1,))) + dot(att[spot, 1], wt[1], ((1,), (1,)))
        for zd in range(8):
            piece = product[zd * 16 : zd * 16 + 16]
            part[r, zd, slot * 16 : slot * 16 + 16] = piece
            if r >= 2:
                direct[r - 2, zd, slot * 16 : slot * 16 + 16] = piece.astype(BF16)

    def rs_copy(r, t, d):
        e = r * 8 + t * 2 + d
        rows = pl.ds(0, 32) if t else pl.ds(16 * d, 16)
        return pltpu.make_async_remote_copy(
            src_ref=sbuf.at[e, rows], dst_ref=rbuf.at[e, rows], send_sem=rs_send.at[e],
            recv_sem=rs_recv.at[e], device_id=(zp, zm)[d], device_id_type=MESH,
        )

    def rs_step(r, t):
        for d in range(2):
            e = r * 8 + t * 2 + d
            dest = (z + 4 - t) % 8 if d == 0 else (z + 4 + t) % 8
            if t == 0:
                rows = pl.ds(16 * d, 16)
                sbuf[e, rows] = part[r, dest, rows].astype(BF16)
            else:
                rs_copy(r, t - 1, d).wait_recv()
                if t == 1:
                    add, own = pl.ds(16 * d, 16), pl.ds(16 - 16 * d, 16)
                    sbuf[e, add] = (part[r, dest, add] + rbuf[e - 2, add].astype(F32)).astype(BF16)
                    sbuf[e, own] = part[r, dest, own].astype(BF16)
                else:
                    sbuf[e] = (part[r, dest] + rbuf[e - 2].astype(F32)).astype(BF16)
            rs_copy(r, t, d).start()

    def d_copy(r, i):
        return pltpu.make_async_remote_copy(
            src_ref=direct.at[r - 2, (z + i) % 8], dst_ref=dbuf.at[r - 2, i - 1], send_sem=d_send.at[r - 2, i - 1],
            recv_sem=d_recv.at[r - 2, i - 1], device_id=(c, ((z + i) % 8) * 2 + yl), device_id_type=MESH,
        )

    def a_copy(r, slot, y2):
        e = r * 4 + slot * 2 + y2
        at = slot * 16 + y2 * 8
        return pltpu.make_async_remote_copy(
            src_ref=fin.at[r, pl.ds(at, 8)], dst_ref=landed.at[c], send_sem=a_send.at[e],
            recv_sem=a_recv.at[c], device_id=(spots(r)[slot] * 2 + yl, z * 2 + y2), device_id_type=MESH,
        )

    def finish(r):
        if r < 2:
            rs_copy(r, 3, 0).wait_recv()
            rs_copy(r, 3, 1).wait_recv()
            fin[r] = part[r, z] + rbuf[r * 8 + 6].astype(F32) + rbuf[r * 8 + 7].astype(F32)
        else:
            total = part[r, z]
            for i in range(1, 8):
                d_copy(r, i).wait_recv()
                total = total + dbuf[r - 2, i - 1].astype(F32)
            fin[r] = total
        for slot in range(2):
            for y2 in range(2):
                if r == 0 and slot == 0:
                    self_copy = (k == yl) & (yl == y2)

                    @pl.when(jnp.logical_not(self_copy))
                    def _():
                        a_copy(r, slot, y2).start()

                    @pl.when(self_copy)
                    def _():
                        landed[c] = fin[r, y2 * 8 : y2 * 8 + 8]
                else:
                    a_copy(r, slot, y2).start()

    arrive3(2)
    start3(10)
    arrive3(4)
    start3(11)
    arrive3(0)
    start3(6, 9)
    arrive3(1)
    start3(8, 7, 15)
    arrive3(3, 5)
    start3(16, 17)
    w_copy.wait_recv()
    arrive3(14)
    project(0, 0)
    arrive3(15)
    project(0, 1)
    rs_step(0, 0)
    arrive3(16, 17)
    project(1, 0)
    project(1, 1)
    rs_step(1, 0)
    arrive3(10, 11)
    start3(20)
    rs_step(0, 1)
    arrive3(6)
    start3(12)
    arrive3(8)
    start3(13)
    rs_step(1, 1)
    rs_step(0, 2)
    arrive3(7, 9)
    start3(18, 19)
    rs_step(1, 2)
    arrive3(18, 19)
    project(2, 0)
    project(2, 1)
    for i in range(1, 8):
        d_copy(2, i).start()
    arrive3(20)
    project(3, 0)
    rs_step(0, 3)
    rs_step(1, 3)
    arrive3(12, 13)
    start3(21)
    arrive3(21)
    project(3, 1)
    for i in range(1, 8):
        d_copy(3, i).start()
    for r in range(4):
        finish(r)

    for c2 in range(16):

        @pl.when(jnp.logical_or(c != c2, yl != k))
        def _():
            pltpu.make_async_remote_copy(
                src_ref=landed.at[c2], dst_ref=landed.at[c2], send_sem=a_send.at[c2],
                recv_sem=a_recv.at[c2], device_id=core, device_id_type=MESH,
            ).wait_recv()

    out_ref[...] = jnp.concatenate([landed[c2] for c2 in range(16)], axis=1).astype(BF16)

    drain1()
    drain3()
    w_copy.wait_send()

    @pl.when(k != yl)
    def _():
        swap(0, True).wait_send()
        swap(1, True).wait_send()

    for r in range(4):
        if r < 2:
            for t in range(4):
                for d in range(2):
                    rs_copy(r, t, d).wait_send()
        else:
            for i in range(1, 8):
                d_copy(r, i).wait_send()
        for slot in range(2):
            for y2 in range(2):

                @pl.when(jnp.logical_not((k == yl) & (yl == y2) & (r == 0) & (slot == 0)))
                def _():
                    a_copy(r, slot, y2).wait_send()


def local(queries, query_rope, latent_cache, key_up, value_up, out_proj):
    dma = pltpu.SemaphoreType.DMA
    return pl.pallas_call(
        kernel,
        out_shape=jax.ShapeDtypeStruct((8, 7168), BF16),
        in_specs=[pl.BlockSpec(memory_space=pl.ANY)] * 6,
        out_specs=pl.BlockSpec(memory_space=pltpu.VMEM),
        scratch_shapes=[
            pltpu.VMEM((BLOCK, HEADS, NOPE), BF16),
            pltpu.VMEM((HEADS, ROPE, BLOCK), BF16),
            pltpu.VMEM((LAT, HEADS * NOPE), BF16),
            pltpu.VMEM((LAT, HEADS * VD), BF16),
            pltpu.VMEM((2, COLS, HEADS * VD), BF16),
            pltpu.VMEM((BLOCK * HEADS, NOPE), F32),
            pltpu.VMEM((BLOCK * HEADS, LAT), BF16),
            pltpu.VMEM((HEADS // 2, ROPE, 2 * BLOCK), BF16),
            pltpu.VMEM((8, 2, LAT + ROPE, BLOCK), BF16),
            pltpu.VMEM((512, LAT + ROPE), BF16),
            pltpu.VMEM((LAT, 512), BF16),
            pltpu.VMEM((4, 1, 256), F32),
            pltpu.VMEM((4, 1, 256), F32),
            pltpu.VMEM((4, LAT, 256), F32),
            pltpu.VMEM((9, 2, BLOCK, HEADS * VD), BF16),
            pltpu.VMEM((4, 8, 32, COLS), F32),
            pltpu.VMEM((2, 8, 32, COLS), BF16),
            pltpu.VMEM((16, 32, COLS), BF16),
            pltpu.VMEM((16, 32, COLS), BF16),
            pltpu.VMEM((2, 7, 32, COLS), BF16),
            pltpu.VMEM((4, 32, COLS), F32),
            pltpu.VMEM((16, 8, COLS), F32),
            dma((6,)), dma((2,)), dma((22,)), dma((22,)), dma((22,)), dma((22,)), dma((2,)), dma((2,)),
            dma((16,)), dma((16,)), dma((2, 7)), dma((2, 7)), dma((16,)), dma((16,)),
        ],
        compiler_params=pltpu.CompilerParams(
            collective_id=0, has_side_effects=True, vmem_limit_bytes=63 * 1024 * 1024
        ),
    )(queries, query_rope.transpose(1, 2, 0), latent_cache.T, key_up, value_up, out_proj.T)


def solution(mesh):
    placed = (
        P("ctx", "head", None),
        P("ctx", "head", None),
        P("ctx", None),
        P(None, "head"),
        P(None, "head"),
        P("head", "ctx"),
    )
    return jax.shard_map(
        local, mesh=mesh, in_specs=placed, out_specs=P(("ctx", "head"), None), check_vma=False
    )
```

```python
import functools

import jax
import jax.numpy as jnp
from jax import lax
from jax.experimental import pallas as pl
from jax.experimental.pallas import tpu as pltpu
from jax.sharding import PartitionSpec as P

LAT = 512
ROPE = 64
NOPE = 128
VD = 128
HEADS = 8
BLOCK = 128
COLS = 448
MASKED = -1e30
LOG2E = 1.4426950408889634
MESH = pl.DeviceIdType.MESH
BF16 = jnp.bfloat16
F32 = jnp.float32


def dot(a, b, contract):
    return lax.dot_general(a, b, ((contract[0], contract[1]), ((), ())), preferred_element_type=F32)


def kernel(
    q_hbm, qrt_hbm, latt_hbm, ku_hbm, vu_hbm, wt_hbm, out_ref,
    q_v, qrt_v, ku_v, vu_v, wt, qf, qa, lt, m_s, l_s, acc, att,
    part, direct, sbuf, rbuf, dbuf, fin, landed,
    loc_sem, w_sem, p1_send, p1_recv, p3_send, p3_recv, swap_send, swap_recv,
    rs_send, rs_recv, d_send, d_recv, a_send, a_recv,
):
    c = lax.axis_index("ctx")
    h = lax.axis_index("head")
    x, yh, k = c // 4, (c // 2) % 2, c % 2
    z, yl = h // 2, h % 2

    def place(dx, flip=False):
        return ((x + dx) % 4) * 2 + ((1 - yh) if flip else yh)

    here = place(0)
    local = [
        pltpu.make_async_copy(src, dst, loc_sem.at[i])
        for i, (src, dst) in enumerate(
            [(latt_hbm, lt.at[here, k]), (q_hbm, q_v), (ku_hbm, ku_v), (qrt_hbm, qrt_v), (vu_hbm, vu_v), (wt_hbm, wt.at[yl])]
        )
    ]
    for copy in local:
        copy.start()

    core = (here * 2 + 1 - k, h)
    xp = (place(1) * 2 + k, h)
    xm = (place(3) * 2 + k, h)
    y_far = (place(0, True) * 2 + k, h)
    y_near = (place(0, True) * 2 + k, z * 2 + 1 - yl)
    y_low = (c, z * 2 + 1 - yl)
    y_cross = (here * 2 + 1 - k, z * 2 + 1 - yl)
    y_near_cross = (place(0, True) * 2 + 1 - k, z * 2 + 1 - yl)
    zp = (c, ((z + 1) % 8) * 2 + yl)
    zm = (c, ((z + 7) % 8) * 2 + yl)

    barrier = pltpu.get_barrier_semaphore()
    greeted = [((c + i) % 16, h) for i in range(1, 16)]
    greeted += [((c + i) % 16, z * 2 + 1 - yl) for i in range(16)]
    greeted += [(c, ((z + i) % 8) * 2 + yl) for i in range(1, 8)]
    for peer in greeted:
        pl.semaphore_signal(barrier, inc=1, device_id=peer, device_id_type=MESH)

    local[1].wait()
    local[2].wait()
    qf[...] = q_v[...].astype(F32).reshape(BLOCK * HEADS, NOPE)
    for i in range(HEADS):
        q_head = qf[pl.ds(i, BLOCK, stride=HEADS), :].astype(BF16)
        absorbed = dot(q_head, ku_v[:, i * NOPE : (i + 1) * NOPE], ((1,), (1,)))
        qa[i * BLOCK : (i + 1) * BLOCK, :LAT] = absorbed.astype(BF16)
    local[3].wait()
    for i in range(HEADS):
        qa[i * BLOCK : (i + 1) * BLOCK, LAT:] = qrt_v[i].T
    local[0].wait()
    local[5].wait()

    pl.semaphore_wait(barrier, len(greeted))

    def gather(at, send, recv, y_peer, last):
        LO, HI, ALL = 0, 1, None
        table = [
            (place(0), LO, y_peer, place(0, True)),
            (place(0), HI, y_peer, place(0, True)),
            (place(0), LO, xp, place(3)),
            (place(0), HI, xp, place(3)),
            (place(0), HI, xm, place(1)),
            (place(0), LO, xm, place(1)),
            (place(0, True), LO, xp, place(3, True)),
            (place(0, True), HI, xp, place(3, True)),
            (place(0, True), HI, xm, place(1, True)),
            (place(0, True), LO, xm, place(1, True)),
            (place(3), LO, xp, place(2)),
            (place(1), HI, xm, place(2)),
        ] + last
        table += [(spot, ALL, core, spot) for spot in (place(0), place(0, True), place(3), place(1), place(3, True), place(1, True), place(2), place(2, True))]

        def copy(e, index):
            _, part_of, peer, _ = table[e]
            slot = (1 - k) if e >= 14 and index == 3 else k
            ref = at(table[e][index], slot, part_of)
            return pltpu.make_async_remote_copy(
                src_ref=ref, dst_ref=ref, send_sem=send.at[e], recv_sem=recv.at[e],
                device_id=peer, device_id_type=MESH,
            )

        def start(*events):
            for e in events:
                copy(e, 0).start()

        def arrive(*events):
            for e in events:
                copy(e, 3).wait_recv()

        def drain():
            for e in range(len(table)):
                copy(e, 0).wait_send()

        return start, arrive, drain

    def latent_at(i, s, half):
        return lt.at[i, s] if half is None else lt.at[i, s, pl.ds(half * 288, 288)]

    def att_at(i, s, half):
        return att.at[i, s] if half is None else att.at[i, s, half]

    by_x = [(place(3, True), 0, xp, place(2, True)), (place(1, True), 1, xm, place(2, True))]
    by_y = [(place(2), 0, y_far, place(2, True)), (place(2), 1, y_far, place(2, True))]
    start1, arrive1, drain1 = gather(latent_at, p1_send, p1_recv, y_near, by_x)
    start3, arrive3, drain3 = gather(att_at, p3_send, p3_recv, y_far, by_x)

    start1(2, 4, 0, 3, 5, 1, 14)

    def w_copy(i):
        rows = (pl.ds(0, 384), pl.ds(384, 64))[i]
        return pltpu.make_async_remote_copy(
            src_ref=wt.at[yl, rows], dst_ref=wt.at[yl, rows], send_sem=w_sem.at[i], recv_sem=w_sem.at[2 + i],
            device_id=y_low, device_id_type=MESH,
        )

    w_copy(0).start()

    def attend(spot, diagonal, first, count):
        rows = pl.ds(first, count)
        keys = jnp.concatenate([lt[spot, 0], lt[spot, 1]], axis=1)
        scores = dot(qa[rows], keys, ((1,), (0,))) * ((NOPE + ROPE) ** -0.5 * LOG2E)
        if diagonal:
            key_pos = lax.broadcasted_iota(jnp.int32, (count, 256), 1)
            query_pos = k * BLOCK + lax.broadcasted_iota(jnp.int32, (count, 256), 0) % BLOCK
            scores = jnp.where(key_pos <= query_pos, scores, MASKED)
            new_max = jnp.broadcast_to(jnp.max(scores, axis=1, keepdims=True), (count, 128))
        else:
            new_max = jnp.maximum(m_s[rows], jnp.max(scores, axis=1, keepdims=True))
        exps = jnp.exp2(scores - jnp.concatenate([new_max] * 2, axis=1))
        sums = exps[:, :128] + exps[:, 128:]
        weighted = dot(exps.astype(BF16), keys[:LAT], ((1,), (1,)))
        if diagonal:
            l_s[rows] = sums
            acc[rows] = weighted
        else:
            rescale = jnp.exp2(m_s[rows] - new_max)
            l_s[rows] = l_s[rows] * rescale + sums
            acc[rows] = acc[rows] * jnp.concatenate([rescale] * 4, axis=1) + weighted
        m_s[rows] = new_max

    def visit(dx, flip, first=0, count=1024):
        spot = place(dx, flip)

        @pl.when(spot < here)
        def _():
            attend(spot, False, first, count)

    arrive1(14)
    attend(here, True, 0, 1024)
    arrive1(2)
    start1(10)
    arrive1(4)
    start1(11)
    arrive1(0)
    start1(6, 9)
    arrive1(1)
    start1(8, 7, 15)
    arrive1(3, 5)
    start1(16, 17)
    arrive1(15)
    visit(0, True)
    arrive1(16)
    visit(3, False)
    arrive1(6)
    start1(12)
    arrive1(8)
    start1(13)
    arrive1(10, 11)
    start1(20)
    arrive1(17)
    visit(1, False)
    arrive1(7, 9)
    start1(18, 19)
    arrive1(20)
    visit(2, False)
    arrive1(12, 13)
    start1(21)
    arrive1(18)
    visit(3, True)
    arrive1(19)
    visit(1, True)
    arrive1(21)
    local[4].wait()

    mine = jnp.where(k == yl, here, 8)

    def swap(half, outgoing):
        return pltpu.make_async_remote_copy(
            src_ref=att.at[8, k, half], dst_ref=att.at[here, (1 - k) if outgoing else k, half],
            send_sem=swap_send.at[half], recv_sem=swap_recv.at[half], device_id=y_cross, device_id_type=MESH,
        )

    def cross(half):
        return pltpu.make_async_remote_copy(
            src_ref=att.at[8, k, half], dst_ref=att.at[here, 1 - k, half], send_sem=p3_send.at[half],
            recv_sem=p3_recv.at[half], device_id=y_near_cross, device_id_type=MESH,
        )

    for half in range(2):
        visit(2, True, 512 * half, 512)

        for i in range(4):
            rows = pl.ds(512 * half + i * BLOCK, BLOCK)
            normed = (acc[rows] / jnp.sum(l_s[rows], axis=1, keepdims=True)).astype(BF16)
            v = (4 * half + i) * VD
            att[mine, k, half, :, i * VD : (i + 1) * VD] = dot(normed, vu_v[:, v : v + VD], ((1,), (0,))).astype(BF16)

        @pl.when(k == yl)
        def _():
            if half == 0:
                start3(2, 5, 0)
            else:
                start3(3, 4, 1, 14)

        @pl.when(k != yl)
        def _():
            swap(half, True).start()
            cross(half).start()

    w_copy(1).start()

    @pl.when(k != yl)
    def _():
        swap(0, False).wait_recv()
        start3(2, 5)
        swap(1, False).wait_recv()
        start3(3, 4, 14)

    rounds = (
        (place(0), place(0, True)), (place(3), place(1)),
        (place(2),), (place(3, True), place(1, True)), (place(2, True),),
    )

    def project(r, slot):
        spot = rounds[r][slot]
        product = sum(
            dot(att[spot, s, half], wt[s, :, half * 512 : half * 512 + 512], ((1,), (1,)))
            for s in range(2) for half in range(2)
        )
        for zd in range(8):
            piece = product[zd * 16 : zd * 16 + 16]
            part[r, zd, slot * 16 : slot * 16 + 16] = piece
            if r >= 2:
                direct[r - 2, zd, slot * 16 : slot * 16 + 16] = piece.astype(BF16)

    def rs_copy(r, t, d):
        e = r * 8 + t * 2 + d
        rows = pl.ds(0, 32) if t else pl.ds(16 * d, 16)
        return pltpu.make_async_remote_copy(
            src_ref=sbuf.at[e, rows], dst_ref=rbuf.at[e, rows], send_sem=rs_send.at[e],
            recv_sem=rs_recv.at[e], device_id=(zp, zm)[d], device_id_type=MESH,
        )

    def rs_step(r, t):
        for d in range(2):
            e = r * 8 + t * 2 + d
            dest = (z + 4 - t) % 8 if d == 0 else (z + 4 + t) % 8
            if t == 0:
                rows = pl.ds(16 * d, 16)
                sbuf[e, rows] = part[r, dest, rows].astype(BF16)
            else:
                rs_copy(r, t - 1, d).wait_recv()
                if t == 1:
                    add, own = pl.ds(16 * d, 16), pl.ds(16 - 16 * d, 16)
                    sbuf[e, add] = (part[r, dest, add] + rbuf[e - 2, add].astype(F32)).astype(BF16)
                    sbuf[e, own] = part[r, dest, own].astype(BF16)
                else:
                    sbuf[e] = (part[r, dest] + rbuf[e - 2].astype(F32)).astype(BF16)
            rs_copy(r, t, d).start()

    def d_copy(r, i):
        rows = pl.ds(0, 16 * len(rounds[r]))
        return pltpu.make_async_remote_copy(
            src_ref=direct.at[r - 2, (z + i) % 8, rows], dst_ref=dbuf.at[r - 2, i - 1, rows], send_sem=d_send.at[r - 2, i - 1],
            recv_sem=d_recv.at[r - 2, i - 1], device_id=(c, ((z + i) % 8) * 2 + yl), device_id_type=MESH,
        )

    def spread(r):
        for i in (4, 3, 5, 2, 6, 1, 7):
            d_copy(r, i).start()

    def a_copy(r, slot, y2):
        e = r * 4 + slot * 2 + y2
        at = slot * 16 + y2 * 8
        return pltpu.make_async_remote_copy(
            src_ref=fin.at[r, pl.ds(at, 8)], dst_ref=landed.at[c], send_sem=a_send.at[e],
            recv_sem=a_recv.at[c], device_id=(rounds[r][slot] * 2 + yl, z * 2 + y2), device_id_type=MESH,
        )

    def finish(r):
        n = 16 * len(rounds[r])
        if r < 2:
            rs_copy(r, 3, 0).wait_recv()
            rs_copy(r, 3, 1).wait_recv()
            fin[r] = part[r, z] + rbuf[r * 8 + 6].astype(F32) + rbuf[r * 8 + 7].astype(F32)
        else:
            total = part[r, z, :n]
            for i in range(1, 8):
                d_copy(r, i).wait_recv()
                total = total + dbuf[r - 2, i - 1, :n].astype(F32)
            fin[r, :n] = total
        for slot in range(len(rounds[r])):
            for y2 in range(2):
                if r == 0 and slot == 0:
                    self_copy = (k == yl) & (yl == y2)

                    @pl.when(jnp.logical_not(self_copy))
                    def _():
                        a_copy(r, slot, y2).start()

                    @pl.when(self_copy)
                    def _():
                        landed[c] = fin[r, y2 * 8 : y2 * 8 + 8]
                else:
                    a_copy(r, slot, y2).start()

    arrive3(2)
    start3(10)
    arrive3(0)
    start3(6, 9)
    arrive3(4)
    start3(11)
    arrive3(1)
    start3(7, 8, 15)
    arrive3(3, 5)
    start3(16, 17)
    drain1()
    w_copy(0).wait_recv()
    w_copy(1).wait_recv()
    arrive3(14)
    project(0, 0)
    arrive3(15)
    project(0, 1)
    rs_step(0, 0)
    arrive3(10, 11)
    start3(20)
    arrive3(16, 17)
    project(1, 0)
    project(1, 1)
    rs_step(1, 0)
    rs_step(0, 1)
    arrive3(20)
    project(2, 0)
    spread(2)
    rs_step(1, 1)
    rs_step(0, 2)
    arrive3(6)
    start3(12)
    arrive3(8)
    start3(13)
    arrive3(7, 9)
    start3(18, 19)
    rs_step(1, 2)
    rs_step(0, 3)
    arrive3(18, 19)
    project(3, 0)
    project(3, 1)
    spread(3)
    arrive3(12, 13)
    start3(21)
    rs_step(1, 3)
    finish(0)
    arrive3(21)
    project(4, 0)
    spread(4)
    finish(1)
    finish(2)
    drain3()
    w_copy(0).wait_send()
    w_copy(1).wait_send()

    @pl.when(k != yl)
    def _():
        swap(0, True).wait_send()
        swap(1, True).wait_send()

    for r in range(2):
        for t in range(4):
            for d in range(2):
                rs_copy(r, t, d).wait_send()
    for i in range(1, 8):
        d_copy(2, i).wait_send()
    finish(3)
    finish(4)

    for c2 in range(16):

        @pl.when(jnp.logical_or(c != c2, yl != k))
        def _():
            pltpu.make_async_remote_copy(
                src_ref=landed.at[c2], dst_ref=landed.at[c2], send_sem=a_send.at[c2],
                recv_sem=a_recv.at[c2], device_id=core, device_id_type=MESH,
            ).wait_recv()

    out_ref[...] = jnp.concatenate([landed[c2] for c2 in range(16)], axis=1).astype(BF16)

    for r in range(5):
        if r >= 3:
            for i in range(1, 8):
                d_copy(r, i).wait_send()
        for slot in range(len(rounds[r])):
            for y2 in range(2):

                @pl.when(jnp.logical_not((k == yl) & (yl == y2) & (r == 0) & (slot == 0)))
                def _():
                    a_copy(r, slot, y2).wait_send()


def local(queries, query_rope, latent_cache, key_up, value_up, out_proj):
    dma = pltpu.SemaphoreType.DMA
    return pl.pallas_call(
        kernel,
        out_shape=jax.ShapeDtypeStruct((8, 7168), BF16),
        in_specs=[pl.BlockSpec(memory_space=pl.ANY)] * 6,
        out_specs=pl.BlockSpec(memory_space=pltpu.VMEM),
        scratch_shapes=[
            pltpu.VMEM((BLOCK, HEADS, NOPE), BF16),
            pltpu.VMEM((HEADS, ROPE, BLOCK), BF16),
            pltpu.VMEM((LAT, HEADS * NOPE), BF16),
            pltpu.VMEM((LAT, HEADS * VD), BF16),
            pltpu.VMEM((2, COLS, HEADS * VD), BF16),
            pltpu.VMEM((BLOCK * HEADS, NOPE), F32),
            pltpu.VMEM((HEADS * BLOCK, LAT + ROPE), BF16),
            pltpu.VMEM((8, 2, LAT + ROPE, BLOCK), BF16),
            pltpu.VMEM((HEADS * BLOCK, 128), F32),
            pltpu.VMEM((HEADS * BLOCK, 128), F32),
            pltpu.VMEM((HEADS * BLOCK, LAT), F32),
            pltpu.VMEM((9, 2, 2, BLOCK, HEADS * VD // 2), BF16),
            pltpu.VMEM((5, 8, 32, COLS), F32),
            pltpu.VMEM((3, 8, 32, COLS), BF16),
            pltpu.VMEM((16, 32, COLS), BF16),
            pltpu.VMEM((16, 32, COLS), BF16),
            pltpu.VMEM((3, 7, 32, COLS), BF16),
            pltpu.VMEM((5, 32, COLS), F32),
            pltpu.VMEM((16, 8, COLS), F32),
            dma((6,)), dma((4,)), dma((22,)), dma((22,)), dma((22,)), dma((22,)), dma((2,)), dma((2,)),
            dma((16,)), dma((16,)), dma((3, 7)), dma((3, 7)), dma((20,)), dma((16,)),
        ],
        compiler_params=pltpu.CompilerParams(
            collective_id=0, has_side_effects=True, vmem_limit_bytes=63 * 1024 * 1024
        ),
    )(queries, query_rope.transpose(1, 2, 0), latent_cache.T, key_up, value_up, out_proj.T)


def solution(mesh):
    placed = (
        P("ctx", "head", None),
        P("ctx", "head", None),
        P("ctx", None),
        P(None, "head"),
        P(None, "head"),
        P("head", "ctx"),
    )
    return jax.shard_map(
        local, mesh=mesh, in_specs=placed, out_specs=P(("ctx", "head"), None), check_vma=False
    )
```

```python
import functools

import jax
import jax.numpy as jnp
from jax import lax
from jax.experimental import pallas as pl
from jax.experimental.pallas import tpu as pltpu
from jax.sharding import PartitionSpec as P

LAT = 512
ROPE = 64
NOPE = 128
VD = 128
HEADS = 8
BLOCK = 128
COLS = 448
MASKED = -1e30
LOG2E = 1.4426950408889634
MESH = pl.DeviceIdType.MESH
BF16 = jnp.bfloat16
F32 = jnp.float32


def dot(a, b, contract):
    return lax.dot_general(a, b, ((contract[0], contract[1]), ((), ())), preferred_element_type=F32)


def kernel(
    q_hbm, qrt_hbm, latt_hbm, ku_hbm, vu_hbm, wt_hbm, out_ref,
    q_v, qrt_v, ku_v, vu_v, wt, qf, qa, lt, m_s, l_s, acc, att,
    part, direct, sbuf, rbuf, dbuf, fin, landed,
    loc_sem, w_sem, p1_send, p1_recv, p3_send, p3_recv, swap_send, swap_recv,
    rs_send, rs_recv, d_send, d_recv, a_send, a_recv,
):
    c = lax.axis_index("ctx")
    h = lax.axis_index("head")
    x, yh, k = c // 4, (c // 2) % 2, c % 2
    z, yl = h // 2, h % 2

    def place(dx, flip=False):
        return ((x + dx) % 4) * 2 + ((1 - yh) if flip else yh)

    here = place(0)
    local = [
        pltpu.make_async_copy(src, dst, loc_sem.at[i])
        for i, (src, dst) in enumerate(
            [(latt_hbm, lt.at[here, k]), (q_hbm, q_v), (ku_hbm, ku_v), (qrt_hbm, qrt_v), (vu_hbm, vu_v), (wt_hbm, wt.at[yl])]
        )
    ]
    for copy in local:
        copy.start()

    core = (here * 2 + 1 - k, h)
    xp = (place(1) * 2 + k, h)
    xm = (place(3) * 2 + k, h)
    y_far = (place(0, True) * 2 + k, h)
    y_near = (place(0, True) * 2 + k, z * 2 + 1 - yl)
    y_low = (c, z * 2 + 1 - yl)
    y_cross = (here * 2 + 1 - k, z * 2 + 1 - yl)
    y_near_cross = (place(0, True) * 2 + 1 - k, z * 2 + 1 - yl)
    zp = (c, ((z + 1) % 8) * 2 + yl)
    zm = (c, ((z + 7) % 8) * 2 + yl)

    barrier = pltpu.get_barrier_semaphore()
    greeted = [((c + i) % 16, h) for i in range(1, 16)]
    greeted += [((c + i) % 16, z * 2 + 1 - yl) for i in range(16)]
    greeted += [(c, ((z + i) % 8) * 2 + yl) for i in range(1, 8)]
    for peer in greeted:
        pl.semaphore_signal(barrier, inc=1, device_id=peer, device_id_type=MESH)

    local[1].wait()
    local[2].wait()
    qf[...] = q_v[...].astype(F32).reshape(BLOCK * HEADS, NOPE)
    for i in range(HEADS):
        q_head = qf[pl.ds(i, BLOCK, stride=HEADS), :].astype(BF16)
        absorbed = dot(q_head, ku_v[:, i * NOPE : (i + 1) * NOPE], ((1,), (1,)))
        qa[i * BLOCK : (i + 1) * BLOCK, :LAT] = absorbed.astype(BF16)
    local[3].wait()
    for i in range(HEADS):
        qa[i * BLOCK : (i + 1) * BLOCK, LAT:] = qrt_v[i].T
    local[0].wait()
    local[5].wait()

    pl.semaphore_wait(barrier, len(greeted))

    def gather(at, send, recv, y_peer, last):
        LO, HI, ALL = 0, 1, None
        table = [
            (place(0), LO, y_peer, place(0, True)),
            (place(0), HI, y_peer, place(0, True)),
            (place(0), LO, xp, place(3)),
            (place(0), HI, xp, place(3)),
            (place(0), HI, xm, place(1)),
            (place(0), LO, xm, place(1)),
            (place(0, True), LO, xp, place(3, True)),
            (place(0, True), HI, xp, place(3, True)),
            (place(0, True), HI, xm, place(1, True)),
            (place(0, True), LO, xm, place(1, True)),
            (place(3), LO, xp, place(2)),
            (place(1), HI, xm, place(2)),
        ] + last
        table += [(spot, ALL, core, spot) for spot in (place(0), place(0, True), place(3), place(1), place(3, True), place(1, True), place(2), place(2, True))]

        def copy(e, index):
            _, part_of, peer, _ = table[e]
            slot = (1 - k) if e >= 14 and index == 3 else k
            ref = at(table[e][index], slot, part_of)
            return pltpu.make_async_remote_copy(
                src_ref=ref, dst_ref=ref, send_sem=send.at[e], recv_sem=recv.at[e],
                device_id=peer, device_id_type=MESH,
            )

        def start(*events):
            for e in events:
                copy(e, 0).start()

        def arrive(*events):
            for e in events:
                copy(e, 3).wait_recv()

        def drain():
            for e in range(len(table)):
                copy(e, 0).wait_send()

        return start, arrive, drain

    def latent_at(i, s, half):
        return lt.at[i, s] if half is None else lt.at[i, s, pl.ds(half * 288, 288)]

    def att_at(i, s, half):
        return att.at[i, s] if half is None else att.at[i, s, half]

    by_x = [(place(3, True), 0, xp, place(2, True)), (place(1, True), 1, xm, place(2, True))]
    by_y = [(place(2), 0, y_far, place(2, True)), (place(2), 1, y_far, place(2, True))]
    start1, arrive1, drain1 = gather(latent_at, p1_send, p1_recv, y_near, by_x)
    start3, arrive3, drain3 = gather(att_at, p3_send, p3_recv, y_far, by_x)

    start1(2, 4, 0, 3, 5, 1, 14)

    def w_copy(i):
        rows = (pl.ds(0, 384), pl.ds(384, 64))[i]
        return pltpu.make_async_remote_copy(
            src_ref=wt.at[yl, rows], dst_ref=wt.at[yl, rows], send_sem=w_sem.at[i], recv_sem=w_sem.at[2 + i],
            device_id=y_low, device_id_type=MESH,
        )

    w_copy(0).start()

    def attend(spot, diagonal, first, count):
        rows = pl.ds(first, count)
        keys = jnp.concatenate([lt[spot, 0], lt[spot, 1]], axis=1)
        scores = dot(qa[rows], keys, ((1,), (0,))) * ((NOPE + ROPE) ** -0.5 * LOG2E)
        if diagonal:
            key_pos = lax.broadcasted_iota(jnp.int32, (count, 256), 1)
            query_pos = k * BLOCK + lax.broadcasted_iota(jnp.int32, (count, 256), 0) % BLOCK
            scores = jnp.where(key_pos <= query_pos, scores, MASKED)
            new_max = jnp.broadcast_to(jnp.max(scores, axis=1, keepdims=True), (count, 128))
        else:
            new_max = jnp.maximum(m_s[rows], jnp.max(scores, axis=1, keepdims=True))
        exps = jnp.exp2(scores - jnp.concatenate([new_max] * 2, axis=1))
        sums = exps[:, :128] + exps[:, 128:]
        weighted = dot(exps.astype(BF16), keys[:LAT], ((1,), (1,)))
        if diagonal:
            l_s[rows] = sums
            acc[rows] = weighted
        else:
            rescale = jnp.exp2(m_s[rows] - new_max)
            l_s[rows] = l_s[rows] * rescale + sums
            acc[rows] = acc[rows] * jnp.concatenate([rescale] * 4, axis=1) + weighted
        m_s[rows] = new_max

    def visit(dx, flip, first=0, count=1024):
        spot = place(dx, flip)

        @pl.when(spot < here)
        def _():
            attend(spot, False, first, count)

    arrive1(14)
    attend(here, True, 0, 1024)
    arrive1(2)
    start1(10)
    arrive1(4)
    start1(11)
    arrive1(0)
    start1(6, 9)
    arrive1(1)
    start1(8, 7, 15)
    arrive1(3, 5)
    start1(16, 17)
    arrive1(15)
    visit(0, True)
    arrive1(16)
    visit(3, False)
    arrive1(6)
    start1(12)
    arrive1(8)
    start1(13)
    arrive1(10, 11)
    start1(20)
    arrive1(17)
    visit(1, False)
    arrive1(7, 9)
    start1(18, 19)
    arrive1(20)
    visit(2, False)
    arrive1(12, 13)
    start1(21)
    arrive1(18)
    visit(3, True, 0, 512)
    arrive1(19)
    visit(1, True, 0, 512)
    arrive1(21)
    local[4].wait()

    mine = jnp.where(k == yl, here, 8)

    def swap(half, outgoing):
        return pltpu.make_async_remote_copy(
            src_ref=att.at[8, k, half], dst_ref=att.at[here, (1 - k) if outgoing else k, half],
            send_sem=swap_send.at[half], recv_sem=swap_recv.at[half], device_id=y_cross, device_id_type=MESH,
        )

    def cross(half):
        return pltpu.make_async_remote_copy(
            src_ref=att.at[8, k, half], dst_ref=att.at[here, 1 - k, half], send_sem=p3_send.at[half],
            recv_sem=p3_recv.at[half], device_id=y_near_cross, device_id_type=MESH,
        )

    for half in range(2):
        if half == 1:
            visit(3, True, 512, 512)
            visit(1, True, 512, 512)
        visit(2, True, 512 * half, 512)

        for i in range(4):
            rows = pl.ds(512 * half + i * BLOCK, BLOCK)
            normed = (acc[rows] / jnp.sum(l_s[rows], axis=1, keepdims=True)).astype(BF16)
            v = (4 * half + i) * VD
            att[mine, k, half, :, i * VD : (i + 1) * VD] = dot(normed, vu_v[:, v : v + VD], ((1,), (0,))).astype(BF16)

        @pl.when(k == yl)
        def _():
            if half == 0:
                start3(2, 5, 0)
            else:
                start3(3, 4, 1, 14)

        @pl.when(k != yl)
        def _():
            cross(half).start()
            swap(half, True).start()

    w_copy(1).start()

    @pl.when(k != yl)
    def _():
        swap(0, False).wait_recv()
        start3(2, 5)
        swap(1, False).wait_recv()
        start3(3, 4, 14)

    rounds = (
        (place(0), place(0, True)), (place(3), place(1)),
        (place(2),), (place(3, True), place(1, True)), (place(2, True),),
    )

    def project(r, slot):
        if slot + 1 < len(rounds[r]) and r in (1, 3):
            return
        both = rounds[r] if r in (1, 3) else (rounds[r][slot],)
        product = 0.0
        for s in range(2):
            for half in range(2):
                rows = jnp.concatenate([att[spot, s, half] for spot in both], axis=0)
                product = product + dot(rows, wt[s, :, half * 512 : half * 512 + 512], ((1,), (1,)))
        for j in range(len(both)):
            to = (j if r in (1, 3) else slot) * 16
            for zd in range(8):
                piece = product[j * BLOCK + zd * 16 : j * BLOCK + zd * 16 + 16]
                part[r, zd, to : to + 16] = piece
                if r >= 2:
                    direct[r - 2, zd, to : to + 16] = piece.astype(BF16)

    def rs_copy(r, t, d):
        e = r * 8 + t * 2 + d
        rows = pl.ds(0, 32) if t else pl.ds(16 * d, 16)
        return pltpu.make_async_remote_copy(
            src_ref=sbuf.at[e, rows], dst_ref=rbuf.at[e, rows], send_sem=rs_send.at[e],
            recv_sem=rs_recv.at[e], device_id=(zp, zm)[d], device_id_type=MESH,
        )

    def rs_step(r, t):
        for d in range(2):
            e = r * 8 + t * 2 + d
            dest = (z + 4 - t) % 8 if d == 0 else (z + 4 + t) % 8
            if t == 0:
                rows = pl.ds(16 * d, 16)
                sbuf[e, rows] = part[r, dest, rows].astype(BF16)
            else:
                rs_copy(r, t - 1, d).wait_recv()
                if t == 1:
                    add, own = pl.ds(16 * d, 16), pl.ds(16 - 16 * d, 16)
                    sbuf[e, add] = (part[r, dest, add] + rbuf[e - 2, add].astype(F32)).astype(BF16)
                    sbuf[e, own] = part[r, dest, own].astype(BF16)
                else:
                    sbuf[e] = (part[r, dest] + rbuf[e - 2].astype(F32)).astype(BF16)
            rs_copy(r, t, d).start()

    def d_copy(r, i):
        rows = pl.ds(0, 16 * len(rounds[r]))
        return pltpu.make_async_remote_copy(
            src_ref=direct.at[r - 2, (z + i) % 8, rows], dst_ref=dbuf.at[r - 2, i - 1, rows], send_sem=d_send.at[r - 2, i - 1],
            recv_sem=d_recv.at[r - 2, i - 1], device_id=(c, ((z + i) % 8) * 2 + yl), device_id_type=MESH,
        )

    def spread(r):
        for i in (4, 3, 5, 2, 6, 1, 7):
            d_copy(r, i).start()

    def a_copy(r, slot, y2):
        e = r * 4 + slot * 2 + y2
        at = slot * 16 + y2 * 8
        return pltpu.make_async_remote_copy(
            src_ref=fin.at[r, pl.ds(at, 8)], dst_ref=landed.at[c], send_sem=a_send.at[e],
            recv_sem=a_recv.at[c], device_id=(rounds[r][slot] * 2 + yl, z * 2 + y2), device_id_type=MESH,
        )

    def finish(r):
        n = 16 * len(rounds[r])
        if r < 2:
            rs_copy(r, 3, 0).wait_recv()
            rs_copy(r, 3, 1).wait_recv()
            fin[r] = part[r, z] + rbuf[r * 8 + 6].astype(F32) + rbuf[r * 8 + 7].astype(F32)
        else:
            total = part[r, z, :n]
            for i in range(1, 8):
                d_copy(r, i).wait_recv()
                total = total + dbuf[r - 2, i - 1, :n].astype(F32)
            fin[r, :n] = total
        for slot in range(len(rounds[r])):
            for y2 in range(2):
                if r == 0 and slot == 0:
                    self_copy = (k == yl) & (yl == y2)

                    @pl.when(jnp.logical_not(self_copy))
                    def _():
                        a_copy(r, slot, y2).start()

                    @pl.when(self_copy)
                    def _():
                        landed[c] = fin[r, y2 * 8 : y2 * 8 + 8]
                else:
                    a_copy(r, slot, y2).start()

    arrive3(2)
    start3(10)
    arrive3(0)
    start3(6, 9)
    arrive3(4)
    start3(11)
    arrive3(1)
    start3(7, 8, 15)
    arrive3(3, 5)
    start3(16, 17)
    drain1()
    w_copy(0).wait_recv()
    w_copy(1).wait_recv()
    arrive3(14)
    project(0, 0)
    arrive3(15)
    project(0, 1)
    rs_step(0, 0)
    arrive3(10, 11)
    start3(20)
    arrive3(16, 17)
    project(1, 0)
    project(1, 1)
    rs_step(1, 0)
    rs_step(0, 1)
    arrive3(20)
    project(2, 0)
    spread(2)
    rs_step(1, 1)
    rs_step(0, 2)
    arrive3(6)
    start3(12)
    arrive3(8)
    start3(13)
    arrive3(7, 9)
    start3(18, 19)
    rs_step(1, 2)
    rs_step(0, 3)
    arrive3(18, 19)
    project(3, 0)
    project(3, 1)
    spread(3)
    arrive3(12, 13)
    start3(21)
    rs_step(1, 3)
    finish(0)
    arrive3(21)
    project(4, 0)
    spread(4)
    finish(1)
    finish(2)
    drain3()
    w_copy(0).wait_send()
    w_copy(1).wait_send()

    @pl.when(k != yl)
    def _():
        swap(0, True).wait_send()
        swap(1, True).wait_send()

    for r in range(2):
        for t in range(4):
            for d in range(2):
                rs_copy(r, t, d).wait_send()
    for i in range(1, 8):
        d_copy(2, i).wait_send()
    finish(3)
    finish(4)

    for r in range(5):
        if r >= 3:
            for i in range(1, 8):
                d_copy(r, i).wait_send()
        for slot in range(len(rounds[r])):
            for y2 in range(2):

                @pl.when(jnp.logical_not((k == yl) & (yl == y2) & (r == 0) & (slot == 0)))
                def _():
                    a_copy(r, slot, y2).wait_send()

    for c2 in range(16):

        @pl.when(jnp.logical_or(c != c2, yl != k))
        def _():
            pltpu.make_async_remote_copy(
                src_ref=landed.at[c2], dst_ref=landed.at[c2], send_sem=a_send.at[c2],
                recv_sem=a_recv.at[c2], device_id=core, device_id_type=MESH,
            ).wait_recv()

    out_ref[...] = jnp.concatenate([landed[c2] for c2 in range(16)], axis=1).astype(BF16)


def local(queries, query_rope, latent_cache, key_up, value_up, out_proj):
    dma = pltpu.SemaphoreType.DMA
    return pl.pallas_call(
        kernel,
        out_shape=jax.ShapeDtypeStruct((8, 7168), BF16),
        in_specs=[pl.BlockSpec(memory_space=pl.ANY)] * 6,
        out_specs=pl.BlockSpec(memory_space=pltpu.VMEM),
        scratch_shapes=[
            pltpu.VMEM((BLOCK, HEADS, NOPE), BF16),
            pltpu.VMEM((HEADS, ROPE, BLOCK), BF16),
            pltpu.VMEM((LAT, HEADS * NOPE), BF16),
            pltpu.VMEM((LAT, HEADS * VD), BF16),
            pltpu.VMEM((2, COLS, HEADS * VD), BF16),
            pltpu.VMEM((BLOCK * HEADS, NOPE), F32),
            pltpu.VMEM((HEADS * BLOCK, LAT + ROPE), BF16),
            pltpu.VMEM((8, 2, LAT + ROPE, BLOCK), BF16),
            pltpu.VMEM((HEADS * BLOCK, 128), F32),
            pltpu.VMEM((HEADS * BLOCK, 128), F32),
            pltpu.VMEM((HEADS * BLOCK, LAT), F32),
            pltpu.VMEM((9, 2, 2, BLOCK, HEADS * VD // 2), BF16),
            pltpu.VMEM((5, 8, 32, COLS), F32),
            pltpu.VMEM((3, 8, 32, COLS), BF16),
            pltpu.VMEM((16, 32, COLS), BF16),
            pltpu.VMEM((16, 32, COLS), BF16),
            pltpu.VMEM((3, 7, 32, COLS), BF16),
            pltpu.VMEM((5, 32, COLS), F32),
            pltpu.VMEM((16, 8, COLS), F32),
            dma((6,)), dma((4,)), dma((22,)), dma((22,)), dma((22,)), dma((22,)), dma((2,)), dma((2,)),
            dma((16,)), dma((16,)), dma((3, 7)), dma((3, 7)), dma((20,)), dma((16,)),
        ],
        compiler_params=pltpu.CompilerParams(
            collective_id=0, has_side_effects=True, vmem_limit_bytes=63 * 1024 * 1024
        ),
    )(queries, query_rope.transpose(1, 2, 0), latent_cache.T, key_up, value_up, out_proj.T)


def solution(mesh):
    placed = (
        P("ctx", "head", None),
        P("ctx", "head", None),
        P("ctx", None),
        P(None, "head"),
        P(None, "head"),
        P("head", "ctx"),
    )
    return jax.shard_map(
        local, mesh=mesh, in_specs=placed, out_specs=P(("ctx", "head"), None), check_vma=False
    )
```

```python
import functools

import jax
import jax.numpy as jnp
from jax import lax
from jax.experimental import pallas as pl
from jax.experimental.pallas import tpu as pltpu
from jax.sharding import PartitionSpec as P

LAT = 512
ROPE = 64
NOPE = 128
VD = 128
HEADS = 8
BLOCK = 128
COLS = 448
MASKED = -1e30
LOG2E = 1.4426950408889634
MESH = pl.DeviceIdType.MESH
BF16 = jnp.bfloat16
F32 = jnp.float32


def dot(a, b, contract):
    return lax.dot_general(a, b, ((contract[0], contract[1]), ((), ())), preferred_element_type=F32)


def kernel(
    q_hbm, qrt_hbm, latt_hbm, ku_hbm, vu_hbm, wt_hbm, out_ref,
    q_v, qrt_v, ku_v, vu_v, wt, qf, qa, lt, m_s, l_s, acc, att,
    part, direct, sbuf, rbuf, dbuf, fin, landed,
    loc_sem, w_sem, p1_send, p1_recv, p3_send, p3_recv, swap_send, swap_recv,
    rs_send, rs_recv, d_send, d_recv, a_send, a_recv,
):
    c = lax.axis_index("ctx")
    h = lax.axis_index("head")
    x, yh, k = c // 4, (c // 2) % 2, c % 2
    z, yl = h // 2, h % 2

    def place(dx, flip=False):
        return ((x + dx) % 4) * 2 + ((1 - yh) if flip else yh)

    here = place(0)
    local = [
        pltpu.make_async_copy(src, dst, loc_sem.at[i])
        for i, (src, dst) in enumerate(
            [(latt_hbm, lt.at[here, k]), (q_hbm, q_v), (ku_hbm, ku_v), (qrt_hbm, qrt_v), (vu_hbm, vu_v), (wt_hbm, wt.at[yl])]
        )
    ]
    for copy in local:
        copy.start()

    core = (here * 2 + 1 - k, h)
    xp = (place(1) * 2 + k, h)
    xm = (place(3) * 2 + k, h)
    y_far = (place(0, True) * 2 + k, h)
    y_near = (place(0, True) * 2 + k, z * 2 + 1 - yl)
    y_low = (c, z * 2 + 1 - yl)
    y_cross = (here * 2 + 1 - k, z * 2 + 1 - yl)
    y_near_cross = (place(0, True) * 2 + 1 - k, z * 2 + 1 - yl)
    zp = (c, ((z + 1) % 8) * 2 + yl)
    zm = (c, ((z + 7) % 8) * 2 + yl)

    barrier = pltpu.get_barrier_semaphore()
    stays = k == yl

    def greet(peers):
        for peer in peers:
            pl.semaphore_signal(barrier, inc=1, device_id=peer, device_id_type=MESH)

    def along(first, head):
        return [((c + i) % 16, head) for i in range(first, 16, 2)]

    greet(along(1, h) + along(0, z * 2 + 1 - yl) + [(c, ((z + i) % 8) * 2 + yl) for i in range(1, 8)])

    @pl.when(stays)
    def _():
        greet(along(2, h))

    @pl.when(jnp.logical_not(stays))
    def _():
        greet(along(1, z * 2 + 1 - yl) + [xp, xm, y_far])

    local[1].wait()
    local[2].wait()
    qf[...] = q_v[...].astype(F32).reshape(BLOCK * HEADS, NOPE)
    for i in range(HEADS):
        q_head = qf[pl.ds(i, BLOCK, stride=HEADS), :].astype(BF16)
        absorbed = dot(q_head, ku_v[:, i * NOPE : (i + 1) * NOPE], ((1,), (1,)))
        qa[i * BLOCK : (i + 1) * BLOCK, :LAT] = absorbed.astype(BF16)
    local[3].wait()
    for i in range(HEADS):
        qa[i * BLOCK : (i + 1) * BLOCK, LAT:] = qrt_v[i].T
    local[0].wait()
    local[5].wait()

    @pl.when(stays)
    def _():
        pl.semaphore_wait(barrier, 30)

    @pl.when(jnp.logical_not(stays))
    def _():
        pl.semaphore_wait(barrier, 34)

    def gather(at, send, recv, y_peer, last):
        LO, HI, ALL = 0, 1, None
        table = [
            (place(0), LO, y_peer, place(0, True)),
            (place(0), HI, y_peer, place(0, True)),
            (place(0), LO, xp, place(3)),
            (place(0), HI, xp, place(3)),
            (place(0), HI, xm, place(1)),
            (place(0), LO, xm, place(1)),
            (place(0, True), LO, xp, place(3, True)),
            (place(0, True), HI, xp, place(3, True)),
            (place(0, True), HI, xm, place(1, True)),
            (place(0, True), LO, xm, place(1, True)),
            (place(3), LO, xp, place(2)),
            (place(1), HI, xm, place(2)),
        ] + last
        table += [(spot, ALL, core, spot) for spot in (place(0), place(0, True), place(3), place(1), place(3, True), place(1, True), place(2), place(2, True))]

        def copy(e, index):
            _, part_of, peer, _ = table[e]
            slot = (1 - k) if e >= 14 and index == 3 else k
            ref = at(table[e][index], slot, part_of)
            return pltpu.make_async_remote_copy(
                src_ref=ref, dst_ref=ref, send_sem=send.at[e], recv_sem=recv.at[e],
                device_id=peer, device_id_type=MESH,
            )

        def start(*events):
            for e in events:
                copy(e, 0).start()

        def arrive(*events):
            for e in events:
                copy(e, 3).wait_recv()

        def drain():
            for e in range(len(table)):
                copy(e, 0).wait_send()

        return start, arrive, drain

    def latent_at(i, s, half):
        return lt.at[i, s] if half is None else lt.at[i, s, pl.ds(half * 288, 288)]

    def att_at(i, s, half):
        return att.at[i, s] if half is None else att.at[i, s, half]

    by_x = [(place(3, True), 0, xp, place(2, True)), (place(1, True), 1, xm, place(2, True))]
    by_both = [(place(3, True), 0, xp, place(2, True)), (place(2), 1, y_far, place(2, True))]
    start1, arrive1, drain1 = gather(latent_at, p1_send, p1_recv, y_near, by_x)
    start3, arrive3, drain3 = gather(att_at, p3_send, p3_recv, y_far, by_both)

    start1(0, 2, 4, 1, 3, 5, 14)

    def w_copy(i):
        rows = (pl.ds(0, 384), pl.ds(384, 64))[i]
        return pltpu.make_async_remote_copy(
            src_ref=wt.at[yl, rows], dst_ref=wt.at[yl, rows], send_sem=w_sem.at[i], recv_sem=w_sem.at[2 + i],
            device_id=y_low, device_id_type=MESH,
        )

    w_copy(0).start()

    def attend(spot, diagonal, first, count):
        rows = pl.ds(first, count)
        keys = jnp.concatenate([lt[spot, 0], lt[spot, 1]], axis=1)
        scores = dot(qa[rows], keys, ((1,), (0,))) * ((NOPE + ROPE) ** -0.5 * LOG2E)
        if diagonal:
            key_pos = lax.broadcasted_iota(jnp.int32, (count, 256), 1)
            query_pos = k * BLOCK + lax.broadcasted_iota(jnp.int32, (count, 256), 0) % BLOCK
            scores = jnp.where(key_pos <= query_pos, scores, MASKED)
            new_max = jnp.broadcast_to(jnp.max(scores, axis=1, keepdims=True), (count, 128))
        else:
            new_max = jnp.maximum(m_s[rows], jnp.max(scores, axis=1, keepdims=True))
        exps = jnp.exp2(scores - jnp.concatenate([new_max] * 2, axis=1))
        sums = exps[:, :128] + exps[:, 128:]
        weighted = dot(exps.astype(BF16), keys[:LAT], ((1,), (1,)))
        if diagonal:
            l_s[rows] = sums
            acc[rows] = weighted
        else:
            rescale = jnp.exp2(m_s[rows] - new_max)
            l_s[rows] = l_s[rows] * rescale + sums
            acc[rows] = acc[rows] * jnp.concatenate([rescale] * 4, axis=1) + weighted
        m_s[rows] = new_max

    def visit(dx, flip, first=0, count=1024):
        spot = place(dx, flip)

        @pl.when(spot < here)
        def _():
            attend(spot, False, first, count)

    arrive1(14)
    attend(here, True, 0, 1024)
    arrive1(2)
    start1(10)
    arrive1(4)
    start1(11)
    arrive1(0)
    start1(6, 9)
    arrive1(1)
    start1(8, 7, 15)
    arrive1(3, 5)
    start1(16, 17)
    arrive1(15)
    visit(0, True)
    arrive1(16)
    visit(3, False)
    arrive1(6)
    start1(12)
    arrive1(8)
    start1(13)
    arrive1(10, 11)
    start1(20)
    arrive1(17)
    visit(1, False)
    arrive1(7, 9)
    start1(18, 19)
    arrive1(20)
    visit(2, False)
    arrive1(12, 13)
    start1(21)
    arrive1(18)
    visit(3, True, 0, 512)
    arrive1(19)
    visit(1, True, 0, 512)
    arrive1(21)
    local[4].wait()

    mine = jnp.where(k == yl, here, 8)

    def swap(half, outgoing):
        return pltpu.make_async_remote_copy(
            src_ref=att.at[8, k, half], dst_ref=att.at[here, (1 - k) if outgoing else k, half],
            send_sem=swap_send.at[half], recv_sem=swap_recv.at[half], device_id=y_cross, device_id_type=MESH,
        )

    def cross(half):
        return pltpu.make_async_remote_copy(
            src_ref=att.at[8, k, half], dst_ref=att.at[here, 1 - k, half], send_sem=p3_send.at[half],
            recv_sem=p3_recv.at[half], device_id=y_near_cross, device_id_type=MESH,
        )

    for half in range(2):
        if half == 1:
            visit(3, True, 512, 512)
            visit(1, True, 512, 512)
        visit(2, True, 512 * half, 512)

        for i in range(4):
            rows = pl.ds(512 * half + i * BLOCK, BLOCK)
            normed = (acc[rows] / jnp.sum(l_s[rows], axis=1, keepdims=True)).astype(BF16)
            v = (4 * half + i) * VD
            att[mine, k, half, :, i * VD : (i + 1) * VD] = dot(normed, vu_v[:, v : v + VD], ((1,), (0,))).astype(BF16)

        @pl.when(k == yl)
        def _():
            if half == 0:
                start3(2, 5, 0)
            else:
                start3(3, 4, 1, 14)

        @pl.when(k != yl)
        def _():
            cross(half).start()
            swap(half, True).start()

    w_copy(1).start()

    @pl.when(k != yl)
    def _():
        swap(0, False).wait_recv()
        start3(2, 5)
        swap(1, False).wait_recv()
        start3(3, 4, 14)

    rounds = (
        (place(0), place(0, True)), (place(3), place(1)),
        (place(2),), (place(3, True), place(1, True)), (place(2, True),),
    )

    def project(r, slot):
        if slot + 1 < len(rounds[r]) and r in (1, 3):
            return
        both = rounds[r] if r in (1, 3) else (rounds[r][slot],)
        product = 0.0
        for s in range(2):
            for half in range(2):
                rows = jnp.concatenate([att[spot, s, half] for spot in both], axis=0)
                product = product + dot(rows, wt[s, :, half * 512 : half * 512 + 512], ((1,), (1,)))
        for j in range(len(both)):
            to = (j if r in (1, 3) else slot) * 16
            for zd in range(8):
                piece = product[j * BLOCK + zd * 16 : j * BLOCK + zd * 16 + 16]
                part[r, zd, to : to + 16] = piece
                if r >= 2:
                    direct[r - 2, zd, to : to + 16] = piece.astype(BF16)

    def rs_copy(r, t, d):
        e = r * 8 + t * 2 + d
        rows = pl.ds(0, 32) if t else pl.ds(16 * d, 16)
        return pltpu.make_async_remote_copy(
            src_ref=sbuf.at[e, rows], dst_ref=rbuf.at[e, rows], send_sem=rs_send.at[e],
            recv_sem=rs_recv.at[e], device_id=(zp, zm)[d], device_id_type=MESH,
        )

    def rs_step(r, t):
        for d in range(2):
            e = r * 8 + t * 2 + d
            dest = (z + 4 - t) % 8 if d == 0 else (z + 4 + t) % 8
            if t == 0:
                rows = pl.ds(16 * d, 16)
                sbuf[e, rows] = part[r, dest, rows].astype(BF16)
            else:
                rs_copy(r, t - 1, d).wait_recv()
                if t == 1:
                    add, own = pl.ds(16 * d, 16), pl.ds(16 - 16 * d, 16)
                    sbuf[e, add] = (part[r, dest, add] + rbuf[e - 2, add].astype(F32)).astype(BF16)
                    sbuf[e, own] = part[r, dest, own].astype(BF16)
                else:
                    sbuf[e] = (part[r, dest] + rbuf[e - 2].astype(F32)).astype(BF16)
            rs_copy(r, t, d).start()

    def d_copy(r, i):
        rows = pl.ds(0, 16 * len(rounds[r]))
        return pltpu.make_async_remote_copy(
            src_ref=direct.at[r - 2, (z + i) % 8, rows], dst_ref=dbuf.at[r - 2, i - 1, rows], send_sem=d_send.at[r - 2, i - 1],
            recv_sem=d_recv.at[r - 2, i - 1], device_id=(c, ((z + i) % 8) * 2 + yl), device_id_type=MESH,
        )

    def spread(r):
        for i in (4, 3, 5, 2, 6, 1, 7):
            d_copy(r, i).start()

    def a_copy(r, slot, y2):
        e = r * 4 + slot * 2 + y2
        at = slot * 16 + y2 * 8
        return pltpu.make_async_remote_copy(
            src_ref=fin.at[r, pl.ds(at, 8)], dst_ref=landed.at[c], send_sem=a_send.at[e],
            recv_sem=a_recv.at[c], device_id=(rounds[r][slot] * 2 + yl, z * 2 + y2), device_id_type=MESH,
        )

    def finish(r):
        n = 16 * len(rounds[r])
        if r < 2:
            rs_copy(r, 3, 0).wait_recv()
            rs_copy(r, 3, 1).wait_recv()
            fin[r] = part[r, z] + rbuf[r * 8 + 6].astype(F32) + rbuf[r * 8 + 7].astype(F32)
        else:
            total = part[r, z, :n]
            for i in range(1, 8):
                d_copy(r, i).wait_recv()
                total = total + dbuf[r - 2, i - 1, :n].astype(F32)
            fin[r, :n] = total
        for slot in range(len(rounds[r])):
            for y2 in range(2):
                if r == 0 and slot == 0:
                    self_copy = (k == yl) & (yl == y2)

                    @pl.when(jnp.logical_not(self_copy))
                    def _():
                        a_copy(r, slot, y2).start()

                    @pl.when(self_copy)
                    def _():
                        landed[c] = fin[r, y2 * 8 : y2 * 8 + 8]
                else:
                    a_copy(r, slot, y2).start()

    arrive3(2)
    start3(10)
    arrive3(0)
    start3(6, 9)
    arrive3(4)
    start3(11)
    arrive3(1)
    start3(7, 8, 15)
    arrive3(3, 5)
    start3(16, 17)
    drain1()
    w_copy(0).wait_recv()
    w_copy(1).wait_recv()
    arrive3(14)
    project(0, 0)
    arrive3(15)
    project(0, 1)
    rs_step(0, 0)
    arrive3(11)
    start3(13)
    arrive3(10)
    start3(20)
    arrive3(16, 17)
    project(1, 0)
    project(1, 1)
    rs_step(1, 0)
    rs_step(0, 1)
    arrive3(20)
    project(2, 0)
    spread(2)
    rs_step(1, 1)
    rs_step(0, 2)
    arrive3(6)
    start3(12)
    arrive3(8, 7, 9)
    start3(18, 19)
    rs_step(1, 2)
    rs_step(0, 3)
    arrive3(18, 19)
    project(3, 0)
    project(3, 1)
    spread(3)
    arrive3(12, 13)
    start3(21)
    rs_step(1, 3)
    finish(0)
    arrive3(21)
    project(4, 0)
    spread(4)
    finish(1)
    finish(2)
    drain3()
    w_copy(0).wait_send()
    w_copy(1).wait_send()

    @pl.when(k != yl)
    def _():
        swap(0, True).wait_send()
        swap(1, True).wait_send()

    for r in range(2):
        for t in range(4):
            for d in range(2):
                rs_copy(r, t, d).wait_send()
    for i in range(1, 8):
        d_copy(2, i).wait_send()
    finish(3)
    finish(4)

    for r in range(5):
        if r >= 3:
            for i in range(1, 8):
                d_copy(r, i).wait_send()
        for slot in range(len(rounds[r])):
            for y2 in range(2):

                @pl.when(jnp.logical_not((k == yl) & (yl == y2) & (r == 0) & (slot == 0)))
                def _():
                    a_copy(r, slot, y2).wait_send()

    for c2 in range(16):

        @pl.when(jnp.logical_or(c != c2, yl != k))
        def _():
            pltpu.make_async_remote_copy(
                src_ref=landed.at[c2], dst_ref=landed.at[c2], send_sem=a_send.at[c2],
                recv_sem=a_recv.at[c2], device_id=core, device_id_type=MESH,
            ).wait_recv()

    out_ref[...] = jnp.concatenate([landed[c2] for c2 in range(16)], axis=1).astype(BF16)


def local(queries, query_rope, latent_cache, key_up, value_up, out_proj):
    dma = pltpu.SemaphoreType.DMA
    return pl.pallas_call(
        kernel,
        out_shape=jax.ShapeDtypeStruct((8, 7168), BF16),
        in_specs=[pl.BlockSpec(memory_space=pl.ANY)] * 6,
        out_specs=pl.BlockSpec(memory_space=pltpu.VMEM),
        scratch_shapes=[
            pltpu.VMEM((BLOCK, HEADS, NOPE), BF16),
            pltpu.VMEM((HEADS, ROPE, BLOCK), BF16),
            pltpu.VMEM((LAT, HEADS * NOPE), BF16),
            pltpu.VMEM((LAT, HEADS * VD), BF16),
            pltpu.VMEM((2, COLS, HEADS * VD), BF16),
            pltpu.VMEM((BLOCK * HEADS, NOPE), F32),
            pltpu.VMEM((HEADS * BLOCK, LAT + ROPE), BF16),
            pltpu.VMEM((8, 2, LAT + ROPE, BLOCK), BF16),
            pltpu.VMEM((HEADS * BLOCK, 128), F32),
            pltpu.VMEM((HEADS * BLOCK, 128), F32),
            pltpu.VMEM((HEADS * BLOCK, LAT), F32),
            pltpu.VMEM((9, 2, 2, BLOCK, HEADS * VD // 2), BF16),
            pltpu.VMEM((5, 8, 32, COLS), F32),
            pltpu.VMEM((3, 8, 32, COLS), BF16),
            pltpu.VMEM((16, 32, COLS), BF16),
            pltpu.VMEM((16, 32, COLS), BF16),
            pltpu.VMEM((3, 7, 32, COLS), BF16),
            pltpu.VMEM((5, 32, COLS), F32),
            pltpu.VMEM((16, 8, COLS), F32),
            dma((6,)), dma((4,)), dma((22,)), dma((22,)), dma((22,)), dma((22,)), dma((2,)), dma((2,)),
            dma((16,)), dma((16,)), dma((3, 7)), dma((3, 7)), dma((20,)), dma((16,)),
        ],
        compiler_params=pltpu.CompilerParams(
            collective_id=0, has_side_effects=True, vmem_limit_bytes=63 * 1024 * 1024
        ),
    )(queries, query_rope.transpose(1, 2, 0), latent_cache.T, key_up, value_up, out_proj.T)


def solution(mesh):
    placed = (
        P("ctx", "head", None),
        P("ctx", "head", None),
        P("ctx", None),
        P(None, "head"),
        P(None, "head"),
        P("head", "ctx"),
    )
    return jax.shard_map(
        local, mesh=mesh, in_specs=placed, out_specs=P(("ctx", "head"), None), check_vma=False
    )
```
